32 devices in a mesh: sect: 4 (over x, core), dom: 8 (over z, y).
Axes of the slice: x: 2, y: 2, z: 4, core: 2. Of those that a mesh axis runs over, the one named last changes fastest.
Arguments:
- face_sens: bfloat16 [4, 4096, 128], P('sect', 'dom'), may hold values from -6 to 6
- face_owner: int32 [4, 4096], P('sect', 'dom'), may hold values from 0 to 7, as said below
- face_node: int32 [4, 4096], P('sect', 'dom'), may hold values from 0 to 8191
- face_mask: int32 [4, 4096], P('sect', 'dom'), may hold values 0 or 1
- adjoint_prev: bfloat16 [32, 128, 64, 128], P('sect', 'dom'), may hold values from -6 to 6
- block_rows: bfloat16 [32, 128, 64, 384], P('sect', 'dom'), may hold values from -0.3 to 1.7
- coupling: int32 [32, 128, 5], P('sect', 'dom'), may hold values from 0 to 23
Outputs:
- adjoint: bfloat16 [32, 128, 64, 128], P('sect', 'dom')
- face_grad: bfloat16 [4, 4096, 128], P('sect', 'dom')
The draws below stay inside these ranges and needn't reach their ends.
Inputs may be any that keep to these rules, and one draw needn't show every extreme that they name: `face_owner`: among the 512 faces of one device at most 128 name the same owner; in every passage one owner is named by exactly 128 faces of every device.
All inputs are finite; a program needn't handle non-finite values. No bound on the sum of `face_mask` on one device may be relied on, other than what follows from the above.
Results may differ from the reference program's by a relative error of at most 0.0062.
Values may be sent and summed in bfloat16 or wider, within the bound.
A program may use at most 128 MiB of HBM per device.

```python
import math
import jax
import jax.numpy as jnp
from jax import lax

SENS = 128
BLK = 64
COUPLED = 5
SWEEPS = 2
BC = 8
BR = 16
FACE_DEV = 512
PASSAGES = 4
CIRC = 32
RAD = 128
FACES = 4096
CAP = 128
NODE_DEV = 8192


def draw_face_owner(key, part):
    key = jax.random.fold_in(key, 3)
    hot_key, pick_key, order_key = jax.random.split(key, 3)
    peer_count = FACES // FACE_DEV
    spare_faces = FACE_DEV - CAP
    hot_owner = jax.random.randint(hot_key, (PASSAGES, 1, 1), 0, peer_count)
    pick_keys = jax.random.split(pick_key, PASSAGES * peer_count)
    chosen = jax.vmap(lambda single: jax.random.permutation(single, (peer_count - 1) * CAP)[:spare_faces])(pick_keys)
    others = (chosen // CAP).reshape(PASSAGES, peer_count, spare_faces)
    others = others + (others >= hot_owner).astype(jnp.int32)
    hot_rows = jnp.broadcast_to(hot_owner, (PASSAGES, peer_count, CAP))
    owners = jnp.concatenate([hot_rows, others], axis=2)
    order_keys = jax.random.split(order_key, PASSAGES * peer_count)
    orders = jax.vmap(lambda single: jax.random.permutation(single, FACE_DEV))(order_keys)
    orders = orders.reshape(PASSAGES, peer_count, FACE_DEV)
    owners = jnp.take_along_axis(owners, orders, axis=2)
    return owners.reshape(PASSAGES, FACES).astype(jnp.int32)


def draw_block_rows(key, part):
    key = jax.random.fold_in(key, 7)
    diag_key, noise_key, off_key = jax.random.split(key, 3)
    tile_shape = (CIRC, RAD, BLK, BLK)
    off_shape = (CIRC, RAD, BLK, COUPLED * BLK)
    off_scale = 0.6 / math.sqrt(COUPLED * BLK)
    gains = jax.random.uniform(diag_key, (CIRC, RAD, BLK, 1), jnp.float32, 0.6, 1.4)
    noise = jax.random.truncated_normal(noise_key, -4.0, 4.0, tile_shape, jnp.float32) * 0.06
    coupled = jax.random.truncated_normal(off_key, -4.0, 4.0, off_shape, jnp.float32) * off_scale
    identity = (lax.broadcasted_iota(jnp.int32, (BLK, BLK), 0) == lax.broadcasted_iota(jnp.int32, (BLK, BLK), 1)).astype(jnp.float32)
    inverse = identity * gains + noise
    return jnp.concatenate([inverse, coupled], axis=-1).astype(jnp.bfloat16)


def with_ends(values, key, least, top_value):
    place = [jax.random.randint(jax.random.fold_in(key, axis), (), 0, length) for axis, length in enumerate(values.shape)]
    longest = values.shape.index(max(values.shape))
    next_to = place[:longest] + [(place[longest] + 1) % values.shape[longest]] + place[longest + 1:]
    return values.at[tuple(place)].set(least).at[tuple(next_to)].set(top_value)


def levels(own_key, extent, cuts, low, high):
    factor_of = 1.0
    for dim, blocks in cuts:
        draws = jax.random.uniform(jax.random.fold_in(jax.random.fold_in(own_key, 6), dim), (blocks,), jnp.float32, low / len(cuts), high / len(cuts))
        factor_of = factor_of * jnp.repeat(jnp.exp(draws), extent[dim] // blocks).reshape((-1,) + (1,) * (len(extent) - 1 - dim))
    return factor_of


def gaussian(stream_key, shape, width, limit, pieces=(), held_as=jnp.bfloat16):
    array = width * jax.random.normal(stream_key, shape, jnp.float32)
    if pieces:
        array = array * levels(stream_key, shape, pieces, -0.22, 0.18)
    return jnp.clip(array, -limit, limit).astype(held_as)


def setup_inputs(seed: int = 0) -> dict:
    seeds = jax.random.split(jax.random.key(seed), 8)
    return {
        "face_sens": gaussian(seeds[0], (PASSAGES, FACES, SENS), 1.0, 6.0, ((0, 4), (1, 8))),
        "face_owner": draw_face_owner(jax.random.fold_in(seeds[7], 71), 0),
        "face_node": with_ends(jax.random.randint(seeds[2], (PASSAGES, FACES), 0, NODE_DEV), jax.random.fold_in(seeds[2], 1), 0, NODE_DEV - 1).astype(jnp.int32),
        "face_mask": with_ends((jax.random.randint(seeds[3], (PASSAGES, FACES), 0, 4) < 3).astype(jnp.int32), jax.random.fold_in(seeds[3], 1), 0, 1),
        "adjoint_prev": gaussian(seeds[4], (CIRC, RAD, BLK, SENS), 1.0, 6.0, ((0, 4), (1, 8))),
        "block_rows": draw_block_rows(jax.random.fold_in(seeds[7], 71), 0),
        "coupling": with_ends(jax.random.randint(seeds[6], (CIRC, RAD, COUPLED), 0, 24), jax.random.fold_in(seeds[6], 1), 0, 23).astype(jnp.int32),
    }


def place_code(code_value):
    position = code_value + (code_value >= 12).astype(jnp.int32)
    return position // 5 - 2, position % 5 - 2


def node_places(face_owner, face_node):
    passage = jnp.arange(PASSAGES, dtype=jnp.int32)[:, None]
    circ_place = passage * BC + face_node // (BR * BLK)
    radial_place = face_owner * BR + (face_node // BLK) % BR
    within = face_node % BLK
    return ((circ_place * RAD + radial_place) * BLK + within).reshape(-1).astype(jnp.int32)


def jacobi_sweep(iterate, node_load, block_rows, coupling):
    wrapped = jnp.concatenate([iterate[-2:], iterate, iterate[:2]], axis=0)
    border = jnp.zeros((CIRC + 4, 2, BLK, SENS), iterate.dtype)
    padded = jnp.concatenate([border, wrapped, border], axis=1)

    def circ_slab(circ_row):
        window = lax.dynamic_slice_in_dim(padded, circ_row, 5, axis=0)
        code_rows = lax.dynamic_index_in_dim(coupling, circ_row, 0, keepdims=False)
        shift_circ, shift_radial = place_code(code_rows)
        radial_index = jnp.arange(RAD, dtype=jnp.int32)[:, None] + 2 + shift_radial
        neighbours = window[2 + shift_circ, radial_index].reshape(RAD, COUPLED * BLK, SENS).astype(jnp.float32)
        tile_rows = lax.dynamic_index_in_dim(block_rows, circ_row, 0, keepdims=False).astype(jnp.float32)
        coupled = jnp.einsum("rij,rjd->rid", tile_rows[:, :, BLK:], neighbours, precision=lax.Precision.HIGHEST)
        slab_load = lax.dynamic_index_in_dim(node_load, circ_row, 0, keepdims=False)
        remainder = lax.optimization_barrier((slab_load - coupled).astype(jnp.bfloat16)).astype(jnp.float32)
        updated = jnp.einsum("rij,rjd->rid", tile_rows[:, :, :BLK], remainder, precision=lax.Precision.HIGHEST)
        return updated.astype(jnp.bfloat16)

    return lax.map(circ_slab, jnp.arange(CIRC, dtype=jnp.int32))


def reference(face_sens, face_owner, face_node, face_mask, adjoint_prev, block_rows, coupling):
    flat_index = node_places(face_owner, face_node)
    live_factor = face_mask.astype(jnp.float32)[:, :, None]
    live_rows = (face_sens.astype(jnp.float32) * live_factor).reshape(-1, SENS)
    node_load = jax.ops.segment_sum(live_rows, flat_index, num_segments=CIRC * RAD * BLK).reshape(CIRC, RAD, BLK, SENS)
    iterate = adjoint_prev
    for sweep_index in range(SWEEPS):
        iterate = jacobi_sweep(iterate, node_load, block_rows, coupling)
    adjoint = iterate
    gathered = jnp.take(adjoint.reshape(-1, SENS), flat_index, axis=0).reshape(PASSAGES, FACES, SENS)
    face_grad = gathered * face_mask.astype(jnp.bfloat16)[:, :, None]
    return adjoint, face_grad
```

```python
import functools

import jax
import jax.numpy as jnp
from jax import lax
from jax.experimental import pallas as pl
from jax.experimental.pallas import tpu as pltpu
from jax.sharding import PartitionSpec as P

MESH = pl.DeviceIdType.MESH
F32 = jnp.float32
BF16 = jnp.bfloat16


def kernel(
    sect_n, dom_n, per_peer,
    sens_ref, owner_ref, node_ref, mask_ref, coupling_ref, adj_ref, block_ref,
    adj_out, grad_out,
    pad0, pad1, tiles, load, final, result, weight,
    rows_send, rows_recv, ids_send, ids_recv, reply_f32, reply_send, reply_recv,
    ids_smem, pick_c, pick_r,
    halo_send, halo_recv, face_send, face_recv, id_send, id_recv, back_send, back_recv,
    local_sem, out_sem,
):
    circ, radial, tile, cols = adj_ref.shape
    codes = coupling_ref.shape[2]
    faces = sens_ref.shape[1]
    span = radial * tile
    slots = dom_n * per_peer
    s = lax.axis_index("sect")
    d = lax.axis_index("dom")
    left = lax.rem(s + sect_n - 1, sect_n)
    right = lax.rem(s + 1, sect_n)
    has_lo = d > 0
    has_hi = d < dom_n - 1

    copy_adj = pltpu.make_async_copy(
        adj_ref, pad0.at[2:circ + 2, 2:radial + 2], local_sem.at[0]
    )
    copy_tiles = pltpu.make_async_copy(block_ref, tiles, local_sem.at[1])
    copy_adj.start()
    copy_tiles.start()

    barrier = pltpu.get_barrier_semaphore()
    for side in (left, right):
        pl.semaphore_signal(barrier, inc=1, device_id={"sect": side}, device_id_type=MESH)
    for k in range(1, dom_n):
        pl.semaphore_signal(
            barrier, inc=1, device_id={"dom": lax.rem(d + k, dom_n)}, device_id_type=MESH
        )

    owner = owner_ref[...]
    peers = max(dom_n, 8)
    hot = lax.broadcasted_iota(jnp.int32, (peers, faces), 0) == owner
    hot_f = hot.astype(F32)
    before = lax.broadcasted_iota(jnp.int32, (faces, faces), 0)
    upto = before <= lax.broadcasted_iota(jnp.int32, (faces, faces), 1)
    count = jnp.dot(
        hot_f.astype(BF16), upto.astype(F32).astype(BF16), preferred_element_type=F32
    )
    rank = jnp.sum(hot_f * (count - 1.0), axis=0, keepdims=True).astype(jnp.int32)
    slot = jnp.where(mask_ref[...] > 0, owner * per_peer + rank, -1)
    node = node_ref[...]
    node_hi = jnp.broadcast_to((node // 64).astype(F32), (8, faces)).astype(BF16)
    node_lo = jnp.broadcast_to((node % 64).astype(F32), (8, faces)).astype(BF16)
    weight[...] = (
        (lax.broadcasted_iota(jnp.int32, (slots, faces), 0) == slot).astype(F32).astype(BF16)
    )
    rows_send[...] = jnp.dot(
        weight[...], sens_ref[0], preferred_element_type=F32
    ).astype(BF16)
    across = (((1,), (1,)), ((), ()))
    for j in range(dom_n):
        if per_peer == 128:
            chosen = weight[j * per_peer:(j + 1) * per_peer, :]
        else:
            place = lax.broadcasted_iota(jnp.int32, (128, faces), 0)
            place = place - lax.rem(d * per_peer, 128)
            inside = (place >= 0) & (place < per_peer) & (place + j * per_peer == slot)
            chosen = inside.astype(F32).astype(BF16)
        high = lax.dot_general(node_hi, chosen, across, preferred_element_type=F32)
        low = lax.dot_general(node_lo, chosen, across, preferred_element_type=F32)
        ids_send[j] = (high * 64.0 + low).astype(jnp.int32)

    pl.semaphore_wait(barrier, dom_n + 1)

    def part(start):
        return pl.ds(pl.multiple_of(start * per_peer, per_peer), per_peer)

    def face_copies(k):
        j = lax.rem(d + k, dom_n)
        ids = pltpu.make_async_remote_copy(
            src_ref=ids_send.at[j], dst_ref=ids_recv.at[d],
            send_sem=id_send.at[k], recv_sem=id_recv.at[k],
            device_id={"dom": j}, device_id_type=MESH,
        )
        rows = pltpu.make_async_remote_copy(
            src_ref=rows_send.at[part(j)], dst_ref=rows_recv.at[part(d)],
            send_sem=face_send.at[k], recv_sem=face_recv.at[k],
            device_id={"dom": j}, device_id_type=MESH,
        )
        return ids, rows

    def back_copy(k):
        j = lax.rem(d + k, dom_n)
        return pltpu.make_async_remote_copy(
            src_ref=reply_send.at[part(j)], dst_ref=reply_recv.at[part(d)],
            send_sem=back_send.at[k], recv_sem=back_recv.at[k],
            device_id={"dom": j}, device_id_type=MESH,
        )

    c_lo, c_hi, c_mid = slice(0, 2), slice(circ - 2, circ), slice(2, circ - 2)

    def shift(piece):
        return slice(piece.start + 2, piece.stop + 2)

    def halo(phase, pad, kind):
        if kind < 2:
            rows = (c_lo, c_hi)[kind]
            source = adj_ref.at[rows] if phase == 0 else pad.at[shift(rows), 2:radial + 2]
            target = pad.at[(slice(circ + 2, circ + 4), slice(0, 2))[kind], 2:radial + 2]
            device = {"sect": (left, right)[kind]}
        elif kind < 8:
            up = kind >= 5
            rows = (c_lo, c_hi, c_mid)[(kind - 2) % 3]
            first = radial - 2 if up else 0
            if phase == 0:
                source = adj_ref.at[rows, first:first + 2]
            else:
                source = pad.at[shift(rows), first + 2:first + 4]
            put = 0 if up else radial + 2
            target = pad.at[shift(rows), put:put + 2]
            device = {"dom": jnp.where(up, jnp.minimum(d + 1, dom_n - 1), jnp.maximum(d - 1, 0))}
        else:
            to_right = (kind - 8) % 2
            put = 0 if kind < 10 else radial + 2
            rows = (c_lo, c_hi)[to_right]
            source = pad.at[shift(rows), put:put + 2]
            target = pad.at[(slice(circ + 2, circ + 4), slice(0, 2))[to_right], put:put + 2]
            device = {"sect": (left, right)[to_right]}
        return pltpu.make_async_remote_copy(
            src_ref=source, dst_ref=target,
            send_sem=halo_send.at[phase, kind], recv_sem=halo_recv.at[phase, kind],
            device_id=device, device_id_type=MESH,
        )

    def start_dom(phase, pad, pieces):
        @pl.when(has_lo)
        def _():
            for kind in pieces:
                halo(phase, pad, 2 + kind).start()

        @pl.when(has_hi)
        def _():
            for kind in pieces:
                halo(phase, pad, 5 + kind).start()

    def forward_corners(phase, pad):
        @pl.when(has_lo)
        def _():
            for kind in (0, 1):
                halo(phase, pad, 5 + kind).wait_recv()
                halo(phase, pad, 8 + kind).start()

        @pl.when(has_hi)
        def _():
            for kind in (0, 1):
                halo(phase, pad, 2 + kind).wait_recv()
                halo(phase, pad, 10 + kind).start()

    def finish_halo(phase, pad):
        for kind in (0, 1):
            halo(phase, pad, kind).wait_recv()

        @pl.when(has_lo)
        def _():
            halo(phase, pad, 7).wait_recv()
            for kind in (8, 9):
                halo(phase, pad, kind).wait_recv()

        @pl.when(has_hi)
        def _():
            halo(phase, pad, 4).wait_recv()
            for kind in (10, 11):
                halo(phase, pad, kind).wait_recv()

    def drain_halo(phase, pad):
        for kind in (0, 1):
            halo(phase, pad, kind).wait_send()

        @pl.when(has_lo)
        def _():
            for kind in (2, 3, 4, 8, 9):
                halo(phase, pad, kind).wait_send()

        @pl.when(has_hi)
        def _():
            for kind in (5, 6, 7, 10, 11):
                halo(phase, pad, kind).wait_send()

    for k in range(1, dom_n):
        for copy in face_copies(k):
            copy.start()
    start_dom(0, pad0, (0, 1))
    for kind in (0, 1):
        halo(0, pad0, kind).start()
    start_dom(0, pad0, (2,))

    ids_recv[d] = ids_send[d]
    rows_recv[part(d), :] = rows_send[part(d), :]
    edge = jnp.zeros((circ + 4, 2, tile, cols), BF16)

    @pl.when(jnp.logical_not(has_lo))
    def _():
        pad0[:, 0:2] = edge
        pad1[:, 0:2] = edge

    @pl.when(jnp.logical_not(has_hi))
    def _():
        pad0[:, radial + 2:radial + 4] = edge
        pad1[:, radial + 2:radial + 4] = edge

    @pl.loop(0, circ * radial)
    def _(b):
        c = b // radial
        r = b % radial
        for k in range(codes):
            value = coupling_ref[c, r, k]
            q = value + (value >= 12).astype(jnp.int32)
            fifth = (q * 13) >> 6
            pick_c[b * codes + k] = c + jnp.clip(fifth, 0, 4)
            pick_r[b * codes + k] = r + jnp.clip(q - 5 * fifth, 0, 4)

    forward_corners(0, pad0)

    for k in range(1, dom_n):
        for copy in face_copies(k):
            copy.wait_recv()
    to_smem = pltpu.make_async_copy(ids_recv, ids_smem, local_sem.at[2])
    to_smem.start()
    groups = []
    share = 128 // per_peer
    for g in range(slots // 128):
        group = ids_recv[g * share][0:1]
        for q in range(1, share):
            group = group + ids_recv[g * share + q][0:1]
        groups.append(group)
    slot_nodes = jnp.concatenate(groups, axis=1)
    chunk = 256

    @pl.loop(0, circ * span // chunk)
    def _(t):
        local = lax.broadcasted_iota(jnp.int32, (chunk, slots), 0)
        hit = (local == slot_nodes - t * chunk).astype(F32).astype(BF16)
        load[pl.ds(pl.multiple_of(t * chunk, chunk), chunk), :] = jnp.dot(
            hit, rows_recv[...], preferred_element_type=F32
        )

    zeros = jnp.zeros((tile, cols), BF16)

    def relax(pad, blocks, store):
        rests = []
        for c, r in blocks:
            b = c * radial + r
            near = [pad[pick_c[b * codes + k], pick_r[b * codes + k]] for k in range(codes)]
            coupled = jnp.dot(
                tiles[c, r], jnp.concatenate([zeros] + near, axis=0),
                preferred_element_type=F32,
            )
            at = pl.ds(pl.multiple_of(b * tile, tile), tile)
            rests.append((load[at, :] - coupled).astype(BF16))
        for (c, r), rest in zip(blocks, rests):
            updated = jnp.dot(
                tiles[c, r, :, 0:2 * tile], jnp.concatenate([rest, zeros], axis=0),
                preferred_element_type=F32,
            ).astype(BF16)
            store(c, r, updated)

    def keep(c, r, value):
        pad1[c + 2, r + 2] = value

    def finish(c, r, value):
        result[c, r] = value
        at = pl.ds(pl.multiple_of((c * radial + r) * tile, tile), tile)
        final[at, :] = value.astype(F32)

    copy_adj.wait()
    copy_tiles.wait()
    finish_halo(0, pad0)
    group = 8
    per_row = radial // group

    @pl.loop(0, 4 * per_row)
    def _(t):
        row = t // per_row
        c = row + (row // 2) * (circ - 4)
        base = (t % per_row) * group
        relax(pad0, [(c, base + i) for i in range(group)], keep)

    start_dom(1, pad1, (0, 1))
    for kind in (0, 1):
        halo(1, pad1, kind).start()

    @pl.loop(2, circ - 2)
    def _(c):
        relax(pad0, [(c, r) for r in (0, 1, radial - 2, radial - 1)], keep)

    start_dom(1, pad1, (2,))

    @pl.loop(0, 2 * (circ - 4))
    def _(t):
        half = (radial - 4) // 2
        base = 2 + (t % 2) * half
        relax(pad0, [(2 + t // 2, base + i) for i in range(half)], keep)

    to_smem.wait()
    forward_corners(1, pad1)
    finish_halo(1, pad1)

    @pl.loop(0, circ * per_row)
    def _(t):
        c = t // per_row
        base = (t % per_row) * group
        relax(pad1, [(c, base + i) for i in range(group)], finish)

    write = pltpu.make_async_copy(result, adj_out, out_sem)
    write.start()

    def gather(j):
        offset = lax.rem(j * per_peer, 128)

        @pl.loop(0, per_peer // 16)
        def _(g):
            for i in range(16):
                p = g * 16 + i
                at = jnp.clip(ids_smem[j, 0, p + offset], 0, circ * span - 1)
                reply_f32[pl.ds(j * per_peer + p, 1), :] = final[pl.ds(at, 1), :]

    for k in range(1, dom_n):
        j = lax.rem(d + k, dom_n)
        gather(j)
        reply_send[part(j), :] = reply_f32[part(j), :].astype(BF16)
        back_copy(k).start()
    gather(d)
    reply_recv[part(d), :] = reply_f32[part(d), :].astype(BF16)

    drain_halo(0, pad0)
    drain_halo(1, pad1)
    for k in range(1, dom_n):
        for copy in face_copies(k):
            copy.wait_send()
    for k in range(1, dom_n):
        back_copy(k).wait()
    grad_out[0] = lax.dot_general(
        weight[...], reply_recv[...], (((0,), (0,)), ((), ())), preferred_element_type=F32
    ).astype(BF16)
    write.wait()


def solution(mesh):
    sect_n, dom_n = mesh.shape["sect"], mesh.shape["dom"]

    def shards(face_sens, face_owner, face_node, face_mask, adjoint_prev, block_rows, coupling):
        circ, radial, tile, cols = adjoint_prev.shape
        faces = face_sens.shape[1]
        per_peer = 2 * faces // dom_n
        slots = per_peer * dom_n
        nodes = circ * radial * tile
        pad = pltpu.VMEM((circ + 4, radial + 4, tile, cols), BF16)
        picks = pltpu.SMEM((circ * radial * coupling.shape[2],), jnp.int32)
        peer_sem = pltpu.SemaphoreType.DMA((dom_n,))
        vmem = pl.BlockSpec(memory_space=pltpu.VMEM)
        anywhere = pl.BlockSpec(memory_space=pl.ANY)
        return pl.pallas_call(
            functools.partial(kernel, sect_n, dom_n, per_peer),
            out_shape=(
                jax.ShapeDtypeStruct(adjoint_prev.shape, BF16),
                jax.ShapeDtypeStruct(face_sens.shape, BF16),
            ),
            in_specs=[vmem, vmem, vmem, vmem, pl.BlockSpec(memory_space=pltpu.SMEM), anywhere, anywhere],
            out_specs=(anywhere, vmem),
            scratch_shapes=[
                pad,
                pad,
                pltpu.VMEM(block_rows.shape, BF16),
                pltpu.VMEM((nodes, cols), F32),
                pltpu.VMEM((nodes, cols), F32),
                pltpu.VMEM(adjoint_prev.shape, BF16),
                pltpu.VMEM((slots, faces), BF16),
                pltpu.VMEM((slots, cols), BF16),
                pltpu.VMEM((slots, cols), BF16),
                pltpu.VMEM((dom_n, 8, 128), jnp.int32),
                pltpu.VMEM((dom_n, 8, 128), jnp.int32),
                pltpu.VMEM((slots, cols), F32),
                pltpu.VMEM((slots, cols), BF16),
                pltpu.VMEM((slots, cols), BF16),
                pltpu.SMEM((dom_n, 8, 128), jnp.int32),
                picks,
                picks,
                pltpu.SemaphoreType.DMA((2, 12)),
                pltpu.SemaphoreType.DMA((2, 12)),
                peer_sem, peer_sem, peer_sem, peer_sem, peer_sem, peer_sem,
                pltpu.SemaphoreType.DMA((3,)),
                pltpu.SemaphoreType.DMA,
            ],
            compiler_params=pltpu.CompilerParams(
                collective_id=0, has_side_effects=True, vmem_limit_bytes=48 * 1024 * 1024
            ),
        )(face_sens, face_owner, face_node, face_mask, coupling, adjoint_prev, block_rows)

    placed = (
        P("sect", "dom", None),
        P("sect", "dom"),
        P("sect", "dom"),
        P("sect", "dom"),
        P("sect", "dom", None, None),
        P("sect", "dom", None, None),
        P("sect", "dom", None),
    )
    return jax.shard_map(
        shards,
        mesh=mesh,
        in_specs=placed,
        out_specs=(P("sect", "dom", None, None), P("sect", "dom", None)),
        check_vma=False,
    )
```

```python
import functools

import jax
import jax.numpy as jnp
from jax import lax
from jax.experimental import pallas as pl
from jax.experimental.pallas import tpu as pltpu
from jax.sharding import PartitionSpec as P

MESH = pl.DeviceIdType.MESH
F32 = jnp.float32
BF16 = jnp.bfloat16


def kernel(
    sect_n, dom_n, per_peer,
    sens_hbm, owner_hbm, node_hbm, mask_hbm, coupling_hbm, adj_ref, block_ref,
    adj_out, grad_out,
    sens_ref, owner_ref, node_ref, mask_ref, coupling_ref, core0, core1,
    pad0, pad1, tiles, load, final, result, weight,
    rows_send, rows_recv, ids_send, ids_recv, reply_f32, reply_send, reply_recv,
    ids_smem, pick_c, pick_r,
    halo_send, halo_recv, face_send, face_recv, id_send, id_recv, back_send, back_recv,
    local_sem, out_sem,
):
    circ, radial, tile, cols = adj_ref.shape
    codes = coupling_ref.shape[0]
    faces = sens_ref.shape[1]
    span = radial * tile
    slots = dom_n * per_peer
    s = lax.axis_index("sect")
    d = lax.axis_index("dom")
    left = lax.rem(s + sect_n - 1, sect_n)
    right = lax.rem(s + 1, sect_n)
    has_lo = d > 0
    has_hi = d < dom_n - 1

    copy_adj = pltpu.make_async_copy(
        adj_ref, pad0.at[2:circ + 2, 2:radial + 2], local_sem.at[0]
    )
    copy_tiles = pltpu.make_async_copy(block_ref, tiles, local_sem.at[1])
    face_in = [
        pltpu.make_async_copy(source, target, local_sem.at[3 + i])
        for i, (source, target) in enumerate((
            (owner_hbm, owner_ref), (mask_hbm, mask_ref), (node_hbm, node_ref),
            (sens_hbm, sens_ref),
        ))
    ]
    for copy in face_in:
        copy.start()
    copy_codes = pltpu.make_async_copy(coupling_hbm, coupling_ref, local_sem.at[7])
    copy_codes.start()
    copy_core = pltpu.make_async_copy(adj_ref, core0, local_sem.at[8])
    copy_core.start()
    copy_adj.start()
    copy_tiles.start()

    barrier = pltpu.get_barrier_semaphore()
    for side in (left, right):
        pl.semaphore_signal(barrier, inc=1, device_id={"sect": side}, device_id_type=MESH)
    for k in range(1, dom_n):
        pl.semaphore_signal(
            barrier, inc=1, device_id={"dom": lax.rem(d + k, dom_n)}, device_id_type=MESH
        )

    for copy in face_in:
        copy.wait()
    owner = owner_ref[...]
    peers = max(dom_n, 8)
    hot = lax.broadcasted_iota(jnp.int32, (peers, faces), 0) == owner
    hot_f = hot.astype(F32)
    before = lax.broadcasted_iota(jnp.int32, (faces, faces), 0)
    upto = before <= lax.broadcasted_iota(jnp.int32, (faces, faces), 1)
    count = jnp.dot(
        hot_f.astype(BF16), upto.astype(F32).astype(BF16), preferred_element_type=F32
    )
    rank = jnp.sum(hot_f * (count - 1.0), axis=0, keepdims=True).astype(jnp.int32)
    slot = jnp.where(mask_ref[...] > 0, owner * per_peer + rank, -1)
    node = node_ref[...]
    node_hi = jnp.broadcast_to((node // 64).astype(F32), (8, faces)).astype(BF16)
    node_lo = jnp.broadcast_to((node % 64).astype(F32), (8, faces)).astype(BF16)
    weight[...] = (
        (lax.broadcasted_iota(jnp.int32, (slots, faces), 0) == slot).astype(F32).astype(BF16)
    )
    rows_send[...] = jnp.dot(
        weight[...], sens_ref[0], preferred_element_type=F32
    ).astype(BF16)
    across = (((1,), (1,)), ((), ()))
    for j in range(dom_n):
        if per_peer == 128:
            chosen = weight[j * per_peer:(j + 1) * per_peer, :]
        else:
            place = lax.broadcasted_iota(jnp.int32, (128, faces), 0)
            place = place - lax.rem(d * per_peer, 128)
            inside = (place >= 0) & (place < per_peer) & (place + j * per_peer == slot)
            chosen = inside.astype(F32).astype(BF16)
        high = lax.dot_general(node_hi, chosen, across, preferred_element_type=F32)
        low = lax.dot_general(node_lo, chosen, across, preferred_element_type=F32)
        ids_send[j] = (high * 64.0 + low).astype(jnp.int32)

    pl.semaphore_wait(barrier, dom_n + 1)

    def part(start):
        return pl.ds(pl.multiple_of(start * per_peer, per_peer), per_peer)

    def face_copies(k):
        j = lax.rem(d + k, dom_n)
        ids = pltpu.make_async_remote_copy(
            src_ref=ids_send.at[j], dst_ref=ids_recv.at[d],
            send_sem=id_send.at[k], recv_sem=id_recv.at[k],
            device_id={"dom": j}, device_id_type=MESH,
        )
        rows = pltpu.make_async_remote_copy(
            src_ref=rows_send.at[part(j)], dst_ref=rows_recv.at[part(d)],
            send_sem=face_send.at[k], recv_sem=face_recv.at[k],
            device_id={"dom": j}, device_id_type=MESH,
        )
        return ids, rows

    def back_copy(k):
        j = lax.rem(d + k, dom_n)
        return pltpu.make_async_remote_copy(
            src_ref=reply_send.at[part(j)], dst_ref=reply_recv.at[part(d)],
            send_sem=back_send.at[k], recv_sem=back_recv.at[k],
            device_id={"dom": j}, device_id_type=MESH,
        )

    c_lo, c_hi, c_mid = slice(0, 2), slice(circ - 2, circ), slice(2, circ - 2)

    def shift(piece):
        return slice(piece.start + 2, piece.stop + 2)

    def halo(phase, pad, kind):
        if kind < 2:
            rows = (c_lo, c_hi)[kind]
            source = adj_ref.at[rows] if phase == 0 else pad.at[shift(rows), 2:radial + 2]
            target = pad.at[(slice(circ + 2, circ + 4), slice(0, 2))[kind], 2:radial + 2]
            device = {"sect": (left, right)[kind]}
        elif kind < 8:
            up = kind >= 5
            rows = (c_lo, c_hi, c_mid)[(kind - 2) % 3]
            first = radial - 2 if up else 0
            if phase == 0:
                source = adj_ref.at[rows, first:first + 2]
            else:
                source = pad.at[shift(rows), first + 2:first + 4]
            put = 0 if up else radial + 2
            target = pad.at[shift(rows), put:put + 2]
            device = {"dom": jnp.where(up, jnp.minimum(d + 1, dom_n - 1), jnp.maximum(d - 1, 0))}
        else:
            to_right = (kind - 8) % 2
            put = 0 if kind < 10 else radial + 2
            rows = (c_lo, c_hi)[to_right]
            source = pad.at[shift(rows), put:put + 2]
            target = pad.at[(slice(circ + 2, circ + 4), slice(0, 2))[to_right], put:put + 2]
            device = {"sect": (left, right)[to_right]}
        return pltpu.make_async_remote_copy(
            src_ref=source, dst_ref=target,
            send_sem=halo_send.at[phase, kind], recv_sem=halo_recv.at[phase, kind],
            device_id=device, device_id_type=MESH,
        )

    def start_dom(phase, pad, pieces):
        @pl.when(has_lo)
        def _():
            for kind in pieces:
                halo(phase, pad, 2 + kind).start()

        @pl.when(has_hi)
        def _():
            for kind in pieces:
                halo(phase, pad, 5 + kind).start()

    def forward_corners(phase, pad):
        @pl.when(has_lo)
        def _():
            for kind in (0, 1):
                halo(phase, pad, 5 + kind).wait_recv()
                halo(phase, pad, 8 + kind).start()

        @pl.when(has_hi)
        def _():
            for kind in (0, 1):
                halo(phase, pad, 2 + kind).wait_recv()
                halo(phase, pad, 10 + kind).start()

    def finish_halo(phase, pad):
        for kind in (0, 1):
            halo(phase, pad, kind).wait_recv()

        @pl.when(has_lo)
        def _():
            halo(phase, pad, 7).wait_recv()
            for kind in (8, 9):
                halo(phase, pad, kind).wait_recv()

        @pl.when(has_hi)
        def _():
            halo(phase, pad, 4).wait_recv()
            for kind in (10, 11):
                halo(phase, pad, kind).wait_recv()

    def drain_halo(phase, pad):
        for kind in (0, 1):
            halo(phase, pad, kind).wait_send()

        @pl.when(has_lo)
        def _():
            for kind in (2, 3, 4, 8, 9):
                halo(phase, pad, kind).wait_send()

        @pl.when(has_hi)
        def _():
            for kind in (5, 6, 7, 10, 11):
                halo(phase, pad, kind).wait_send()

    for k in range(1, dom_n):
        for copy in face_copies(k):
            copy.start()
    start_dom(0, pad0, (0, 1))
    for kind in (0, 1):
        halo(0, pad0, kind).start()
    start_dom(0, pad0, (2,))

    ids_recv[d] = ids_send[d]
    rows_recv[part(d), :] = rows_send[part(d), :]
    edge = jnp.zeros((circ + 4, 2, tile, cols), BF16)

    @pl.when(jnp.logical_not(has_lo))
    def _():
        pad0[:, 0:2] = edge
        pad1[:, 0:2] = edge

    @pl.when(jnp.logical_not(has_hi))
    def _():
        pad0[:, radial + 2:radial + 4] = edge
        pad1[:, radial + 2:radial + 4] = edge

    copy_codes.wait()

    @pl.loop(0, circ * radial)
    def _(b):
        c = b // radial
        r = b % radial
        for k in range(codes):
            value = coupling_ref[k, c, r]
            q = value + (value >= 12).astype(jnp.int32)
            fifth = (q * 13) >> 6
            pick_c[b * codes + k] = c + jnp.clip(fifth, 0, 4)
            pick_r[b * codes + k] = r + jnp.clip(q - 5 * fifth, 0, 4)

    forward_corners(0, pad0)

    for k in range(1, dom_n):
        for copy in face_copies(k):
            copy.wait_recv()
    to_smem = pltpu.make_async_copy(ids_recv, ids_smem, local_sem.at[2])
    to_smem.start()
    groups = []
    share = 128 // per_peer
    for g in range(slots // 128):
        group = ids_recv[g * share][0:1]
        for q in range(1, share):
            group = group + ids_recv[g * share + q][0:1]
        groups.append(group)
    slot_nodes = jnp.concatenate(groups, axis=1)
    chunk = 256

    @pl.loop(0, circ * span // chunk)
    def _(t):
        local = lax.broadcasted_iota(jnp.int32, (chunk, slots), 0)
        hit = (local == slot_nodes - t * chunk).astype(F32).astype(BF16)
        load[pl.ds(pl.multiple_of(t * chunk, chunk), chunk), :] = jnp.dot(
            hit, rows_recv[...], preferred_element_type=F32
        )

    zeros = jnp.zeros((tile, cols), BF16)

    def relax(pad, blocks, store, less=0):
        rests = []
        for c, r in blocks:
            b = c * radial + r
            near = [
                pad[pick_c[b * codes + k] - less, pick_r[b * codes + k] - less]
                for k in range(codes)
            ]
            coupled = jnp.dot(
                tiles[c, r], jnp.concatenate([zeros] + near, axis=0),
                preferred_element_type=F32,
            )
            at = pl.ds(pl.multiple_of(b * tile, tile), tile)
            rests.append((load[at, :] - coupled).astype(BF16))
        for (c, r), rest in zip(blocks, rests):
            updated = jnp.dot(
                tiles[c, r, :, 0:2 * tile], jnp.concatenate([rest, zeros], axis=0),
                preferred_element_type=F32,
            ).astype(BF16)
            store(c, r, updated)

    def keep(c, r, value):
        pad1[c + 2, r + 2] = value
        core1[c, r] = value

    def finish(c, r, value):
        result[c, r] = value
        at = pl.ds(pl.multiple_of((c * radial + r) * tile, tile), tile)
        final[at, :] = value.astype(F32)

    def inner_blocks(core, store):
        half = (radial - 4) // 2

        @pl.loop(0, 2 * (circ - 4))
        def _(t):
            base = 2 + (t % 2) * half
            relax(core, [(2 + t // 2, base + i) for i in range(half)], store, 2)

    group = 8
    per_row = radial // group

    def outer_rows(pad, store):
        @pl.loop(0, 4 * per_row)
        def _(t):
            row = t // per_row
            c = row + (row // 2) * (circ - 4)
            base = (t % per_row) * group
            relax(pad, [(c, base + i) for i in range(group)], store)

    def outer_columns(pad, store):
        @pl.loop(1, circ // 2 - 1)
        def _(t):
            ends = (0, 1, radial - 2, radial - 1)
            relax(pad, [(2 * t + i, r) for i in range(2) for r in ends], store)

    copy_core.wait()
    copy_tiles.wait()
    inner_blocks(core0, keep)
    copy_adj.wait()
    finish_halo(0, pad0)
    outer_rows(pad0, keep)
    start_dom(1, pad1, (0, 1))
    for kind in (0, 1):
        halo(1, pad1, kind).start()
    outer_columns(pad0, keep)
    start_dom(1, pad1, (2,))
    to_smem.wait()
    inner_blocks(core1, finish)
    forward_corners(1, pad1)
    finish_halo(1, pad1)
    outer_rows(pad1, finish)
    outer_columns(pad1, finish)

    write = pltpu.make_async_copy(result, adj_out, out_sem)
    write.start()

    def gather(j):
        offset = lax.rem(j * per_peer, 128)

        @pl.loop(0, per_peer // 16)
        def _(g):
            for i in range(16):
                p = g * 16 + i
                at = jnp.clip(ids_smem[j, 0, p + offset], 0, circ * span - 1)
                reply_f32[pl.ds(j * per_peer + p, 1), :] = final[pl.ds(at, 1), :]

    for k in range(1, dom_n):
        j = lax.rem(d + k, dom_n)
        gather(j)
        reply_send[part(j), :] = reply_f32[part(j), :].astype(BF16)
        back_copy(k).start()
    gather(d)
    reply_recv[part(d), :] = reply_f32[part(d), :].astype(BF16)

    drain_halo(0, pad0)
    drain_halo(1, pad1)
    for k in range(1, dom_n):
        for copy in face_copies(k):
            copy.wait_send()
    for k in range(1, dom_n):
        back_copy(k).wait()
    grad_out[0] = lax.dot_general(
        weight[...], reply_recv[...], (((0,), (0,)), ((), ())), preferred_element_type=F32
    ).astype(BF16)
    write.wait()


def solution(mesh):
    sect_n, dom_n = mesh.shape["sect"], mesh.shape["dom"]

    def shards(face_sens, face_owner, face_node, face_mask, adjoint_prev, block_rows, coupling):
        circ, radial, tile, cols = adjoint_prev.shape
        faces = face_sens.shape[1]
        per_peer = 2 * faces // dom_n
        slots = per_peer * dom_n
        nodes = circ * radial * tile
        pad = pltpu.VMEM((circ + 4, radial + 4, tile, cols), BF16)
        picks = pltpu.SMEM((circ * radial * coupling.shape[2],), jnp.int32)
        peer_sem = pltpu.SemaphoreType.DMA((dom_n,))
        vmem = pl.BlockSpec(memory_space=pltpu.VMEM)
        anywhere = pl.BlockSpec(memory_space=pl.ANY)
        codes = jnp.transpose(coupling, (2, 0, 1))
        return pl.pallas_call(
            functools.partial(kernel, sect_n, dom_n, per_peer),
            out_shape=(
                jax.ShapeDtypeStruct(adjoint_prev.shape, BF16),
                jax.ShapeDtypeStruct(face_sens.shape, BF16),
            ),
            in_specs=[anywhere] * 7,
            out_specs=(anywhere, vmem),
            scratch_shapes=[
                pltpu.VMEM(face_sens.shape, BF16),
                pltpu.VMEM(face_owner.shape, jnp.int32),
                pltpu.VMEM(face_owner.shape, jnp.int32),
                pltpu.VMEM(face_owner.shape, jnp.int32),
                pltpu.SMEM((coupling.shape[2], circ, radial), jnp.int32),
                pltpu.VMEM(adjoint_prev.shape, BF16),
                pltpu.VMEM(adjoint_prev.shape, BF16),
                pad,
                pad,
                pltpu.VMEM(block_rows.shape, BF16),
                pltpu.VMEM((nodes, cols), F32),
                pltpu.VMEM((nodes, cols), F32),
                pltpu.VMEM(adjoint_prev.shape, BF16),
                pltpu.VMEM((slots, faces), BF16),
                pltpu.VMEM((slots, cols), BF16),
                pltpu.VMEM((slots, cols), BF16),
                pltpu.VMEM((dom_n, 8, 128), jnp.int32),
                pltpu.VMEM((dom_n, 8, 128), jnp.int32),
                pltpu.VMEM((slots, cols), F32),
                pltpu.VMEM((slots, cols), BF16),
                pltpu.VMEM((slots, cols), BF16),
                pltpu.SMEM((dom_n, 8, 128), jnp.int32),
                picks,
                picks,
                pltpu.SemaphoreType.DMA((2, 12)),
                pltpu.SemaphoreType.DMA((2, 12)),
                peer_sem, peer_sem, peer_sem, peer_sem, peer_sem, peer_sem,
                pltpu.SemaphoreType.DMA((9,)),
                pltpu.SemaphoreType.DMA,
            ],
            compiler_params=pltpu.CompilerParams(
                collective_id=0, has_side_effects=True, vmem_limit_bytes=60 * 1024 * 1024
            ),
        )(face_sens, face_owner, face_node, face_mask, codes, adjoint_prev, block_rows)

    placed = (
        P("sect", "dom", None),
        P("sect", "dom"),
        P("sect", "dom"),
        P("sect", "dom"),
        P("sect", "dom", None, None),
        P("sect", "dom", None, None),
        P("sect", "dom", None),
    )
    return jax.shard_map(
        shards,
        mesh=mesh,
        in_specs=placed,
        out_specs=(P("sect", "dom", None, None), P("sect", "dom", None)),
        check_vma=False,
    )
```

```python
import functools

import jax
import jax.numpy as jnp
from jax import lax
from jax.experimental import pallas as pl
from jax.experimental.pallas import tpu as pltpu
from jax.sharding import PartitionSpec as P

MESH = pl.DeviceIdType.MESH
F32 = jnp.float32
BF16 = jnp.bfloat16


def partner(index, k):
    other = index
    bit = 1
    while bit <= k:
        if k & bit:
            other = other + bit * (1 - 2 * ((index // bit) % 2))
        bit *= 2
    return other


def kernel(
    sect_n, dom_n, per_peer,
    sens_hbm, owner_hbm, node_hbm, mask_hbm, coupling_hbm, adj_ref, block_ref,
    adj_out, grad_out,
    sens_ref, owner_ref, node_ref, mask_ref, coupling_ref, core0, core1,
    pad0, pad1, tiles, load, final, result, weight,
    rows_send, rows_recv, ids_send, ids_recv, reply_f32, reply_send, reply_recv,
    ids_smem, pick_c, pick_r,
    halo_send, halo_recv, face_send, face_recv, id_send, id_recv, back_send, back_recv,
    local_sem, out_sem,
):
    circ, radial, tile, cols = adj_ref.shape
    codes = coupling_ref.shape[0]
    faces = sens_ref.shape[1]
    span = radial * tile
    slots = dom_n * per_peer
    s = lax.axis_index("sect")
    d = lax.axis_index("dom")
    left = lax.rem(s + sect_n - 1, sect_n)
    right = lax.rem(s + 1, sect_n)
    has_lo = d > 0
    has_hi = d < dom_n - 1

    copy_adj = pltpu.make_async_copy(
        adj_ref, pad0.at[2:circ + 2, 2:radial + 2], local_sem.at[0]
    )
    copy_tiles = pltpu.make_async_copy(block_ref, tiles, local_sem.at[1])
    face_in = [
        pltpu.make_async_copy(source, target, local_sem.at[3 + i])
        for i, (source, target) in enumerate((
            (owner_hbm, owner_ref), (mask_hbm, mask_ref), (node_hbm, node_ref),
            (sens_hbm, sens_ref),
        ))
    ]
    for copy in face_in:
        copy.start()
    copy_codes = pltpu.make_async_copy(coupling_hbm, coupling_ref, local_sem.at[7])
    copy_codes.start()
    copy_core = pltpu.make_async_copy(adj_ref, core0, local_sem.at[8])
    copy_core.start()
    copy_adj.start()
    copy_tiles.start()

    barrier = pltpu.get_barrier_semaphore()
    for side in (left, right):
        pl.semaphore_signal(barrier, inc=1, device_id={"sect": side}, device_id_type=MESH)
    for k in range(1, dom_n):
        pl.semaphore_signal(
            barrier, inc=1, device_id={"dom": lax.rem(d + k, dom_n)}, device_id_type=MESH
        )

    for copy in face_in:
        copy.wait()
    owner = owner_ref[...]
    peers = max(dom_n, 8)
    hot = lax.broadcasted_iota(jnp.int32, (peers, faces), 0) == owner
    hot_f = hot.astype(F32)
    before = lax.broadcasted_iota(jnp.int32, (faces, faces), 0)
    upto = before <= lax.broadcasted_iota(jnp.int32, (faces, faces), 1)
    count = jnp.dot(
        hot_f.astype(BF16), upto.astype(F32).astype(BF16), preferred_element_type=F32
    )
    rank = jnp.sum(hot_f * (count - 1.0), axis=0, keepdims=True).astype(jnp.int32)
    slot = jnp.where(mask_ref[...] > 0, owner * per_peer + rank, -1)
    node = node_ref[...]
    node_hi = jnp.broadcast_to((node // 64).astype(F32), (8, faces)).astype(BF16)
    node_lo = jnp.broadcast_to((node % 64).astype(F32), (8, faces)).astype(BF16)
    weight[...] = (
        (lax.broadcasted_iota(jnp.int32, (slots, faces), 0) == slot).astype(F32).astype(BF16)
    )
    rows_send[...] = jnp.dot(
        weight[...], sens_ref[0], preferred_element_type=F32
    ).astype(BF16)
    across = (((1,), (1,)), ((), ()))
    for k in range(dom_n):
        j = partner(d, k)
        if per_peer == 128:
            chosen = weight[pl.ds(pl.multiple_of(j * per_peer, per_peer), per_peer), :]
        else:
            place = lax.broadcasted_iota(jnp.int32, (128, faces), 0) - k * per_peer % 128
            inside = (place >= 0) & (place < per_peer) & (place + j * per_peer == slot)
            chosen = inside.astype(F32).astype(BF16)
        high = lax.dot_general(node_hi, chosen, across, preferred_element_type=F32)
        low = lax.dot_general(node_lo, chosen, across, preferred_element_type=F32)
        ids_send[k] = (high * 64.0 + low).astype(jnp.int32)

    pl.semaphore_wait(barrier, dom_n + 1)

    def part(start):
        if isinstance(start, int):
            return pl.ds(start * per_peer, per_peer)
        return pl.ds(pl.multiple_of(start * per_peer, per_peer), per_peer)

    def face_copies(k):
        j = partner(d, k)
        ids = pltpu.make_async_remote_copy(
            src_ref=ids_send.at[k], dst_ref=ids_recv.at[k],
            send_sem=id_send.at[k], recv_sem=id_recv.at[k],
            device_id={"dom": j}, device_id_type=MESH,
        )
        rows = pltpu.make_async_remote_copy(
            src_ref=rows_send.at[part(j)], dst_ref=rows_recv.at[part(k)],
            send_sem=face_send.at[k], recv_sem=face_recv.at[k],
            device_id={"dom": j}, device_id_type=MESH,
        )
        return ids, rows

    def back_copy(k):
        return pltpu.make_async_remote_copy(
            src_ref=reply_send.at[part(k)], dst_ref=reply_recv.at[part(d)],
            send_sem=back_send.at[k], recv_sem=back_recv.at[k],
            device_id={"dom": partner(d, k)}, device_id_type=MESH,
        )

    c_lo, c_hi, c_mid = slice(0, 2), slice(circ - 2, circ), slice(2, circ - 2)

    def shift(piece):
        return slice(piece.start + 2, piece.stop + 2)

    def halo(phase, pad, kind):
        if kind < 2:
            rows = (c_lo, c_hi)[kind]
            source = adj_ref.at[rows] if phase == 0 else pad.at[shift(rows), 2:radial + 2]
            target = pad.at[(slice(circ + 2, circ + 4), slice(0, 2))[kind], 2:radial + 2]
            device = {"sect": (left, right)[kind]}
        elif kind < 8:
            up = kind >= 5
            rows = (c_lo, c_hi, c_mid)[(kind - 2) % 3]
            first = radial - 2 if up else 0
            if phase == 0:
                source = adj_ref.at[rows, first:first + 2]
            else:
                source = pad.at[shift(rows), first + 2:first + 4]
            put = 0 if up else radial + 2
            target = pad.at[shift(rows), put:put + 2]
            device = {"dom": jnp.where(up, jnp.minimum(d + 1, dom_n - 1), jnp.maximum(d - 1, 0))}
        else:
            to_right = (kind - 8) % 2
            put = 0 if kind < 10 else radial + 2
            rows = (c_lo, c_hi)[to_right]
            source = pad.at[shift(rows), put:put + 2]
            target = pad.at[(slice(circ + 2, circ + 4), slice(0, 2))[to_right], put:put + 2]
            device = {"sect": (left, right)[to_right]}
        return pltpu.make_async_remote_copy(
            src_ref=source, dst_ref=target,
            send_sem=halo_send.at[phase, kind], recv_sem=halo_recv.at[phase, kind],
            device_id=device, device_id_type=MESH,
        )

    def start_dom(phase, pad, pieces):
        @pl.when(has_lo)
        def _():
            for kind in pieces:
                halo(phase, pad, 2 + kind).start()

        @pl.when(has_hi)
        def _():
            for kind in pieces:
                halo(phase, pad, 5 + kind).start()

    def forward_corners(phase, pad):
        @pl.when(has_lo)
        def _():
            for kind in (0, 1):
                halo(phase, pad, 5 + kind).wait_recv()
                halo(phase, pad, 8 + kind).start()

        @pl.when(has_hi)
        def _():
            for kind in (0, 1):
                halo(phase, pad, 2 + kind).wait_recv()
                halo(phase, pad, 10 + kind).start()

    def finish_halo(phase, pad):
        for kind in (0, 1):
            halo(phase, pad, kind).wait_recv()

        @pl.when(has_lo)
        def _():
            halo(phase, pad, 7).wait_recv()
            for kind in (8, 9):
                halo(phase, pad, kind).wait_recv()

        @pl.when(has_hi)
        def _():
            halo(phase, pad, 4).wait_recv()
            for kind in (10, 11):
                halo(phase, pad, kind).wait_recv()

    def drain_halo(phase, pad):
        for kind in (0, 1):
            halo(phase, pad, kind).wait_send()

        @pl.when(has_lo)
        def _():
            for kind in (2, 3, 4, 8, 9):
                halo(phase, pad, kind).wait_send()

        @pl.when(has_hi)
        def _():
            for kind in (5, 6, 7, 10, 11):
                halo(phase, pad, kind).wait_send()

    for k in reversed(range(1, dom_n)):
        for copy in face_copies(k):
            copy.start()
    start_dom(0, pad0, (0, 1))
    for kind in (0, 1):
        halo(0, pad0, kind).start()
    start_dom(0, pad0, (2,))

    ids_recv[0] = ids_send[0]
    rows_recv[part(0), :] = rows_send[part(d), :]
    edge = jnp.zeros((circ + 4, 2, tile, cols), BF16)

    @pl.when(jnp.logical_not(has_lo))
    def _():
        pad0[:, 0:2] = edge
        pad1[:, 0:2] = edge

    @pl.when(jnp.logical_not(has_hi))
    def _():
        pad0[:, radial + 2:radial + 4] = edge
        pad1[:, radial + 2:radial + 4] = edge

    copy_codes.wait()

    @pl.loop(0, circ * radial)
    def _(b):
        c = b // radial
        r = b % radial
        for k in range(codes):
            value = coupling_ref[k, c, r]
            q = value + (value >= 12).astype(jnp.int32)
            fifth = (q * 13) >> 6
            pick_c[b * codes + k] = c + jnp.clip(fifth, 0, 4)
            pick_r[b * codes + k] = r + jnp.clip(q - 5 * fifth, 0, 4)

    chunk = 1024
    half_n = dom_n // 2
    wide = slots // 2

    def face_sums(near):
        base = 0 if near else half_n
        for k in range(max(base, 1), base + half_n):
            for copy in face_copies(k):
                copy.wait_recv()
        groups = []
        share = 128 // per_peer
        for g in range(wide // 128):
            group = ids_recv[base + g * share][0:1]
            for q in range(1, share):
                group = group + ids_recv[base + g * share + q][0:1]
            groups.append(group)
        slot_nodes = jnp.concatenate(groups, axis=1)
        local = lax.broadcasted_iota(jnp.int32, (chunk, wide), 0).astype(jnp.int32)

        @pl.loop(0, circ * span // chunk)
        def _(t):
            offset = slot_nodes - t * chunk
            hit = (local == offset).astype(F32).astype(BF16)
            at = pl.ds(pl.multiple_of(t * chunk, chunk), chunk)
            total = jnp.dot(
                hit, rows_recv[base * per_peer:base * per_peer + wide, :],
                preferred_element_type=F32,
            )
            load[at, :] = total if near else load[at, :] + total

    face_sums(True)
    forward_corners(0, pad0)
    face_sums(False)
    to_smem = pltpu.make_async_copy(ids_recv, ids_smem, local_sem.at[2])
    to_smem.start()

    zeros = jnp.zeros((tile, cols), BF16)

    def relax(pad, blocks, store, less=0):
        rests = []
        for c, r in blocks:
            b = c * radial + r
            near = [
                pad[pick_c[b * codes + k] - less, pick_r[b * codes + k] - less]
                for k in range(codes)
            ]
            coupled = jnp.dot(
                tiles[c, r], jnp.concatenate([zeros] + near, axis=0),
                preferred_element_type=F32,
            )
            at = pl.ds(pl.multiple_of(b * tile, tile), tile)
            rests.append((load[at, :] - coupled).astype(BF16))
        for (c, r), rest in zip(blocks, rests):
            updated = jnp.dot(
                tiles[c, r, :, 0:2 * tile], jnp.concatenate([rest, zeros], axis=0),
                preferred_element_type=F32,
            ).astype(BF16)
            store(c, r, updated)

    def keep(c, r, value):
        pad1[c + 2, r + 2] = value
        core1[c, r] = value

    def finish(c, r, value):
        result[c, r] = value
        at = pl.ds(pl.multiple_of((c * radial + r) * tile, tile), tile)
        final[at, :] = value.astype(F32)

    def inner_blocks(core, store):
        half = (radial - 4) // 2

        @pl.loop(0, 2 * (circ - 4))
        def _(t):
            base = 2 + (t % 2) * half
            relax(core, [(2 + t // 2, base + i) for i in range(half)], store, 2)

    group = 8
    per_row = radial // group

    def outer_rows(pad, store):
        @pl.loop(0, 4 * per_row)
        def _(t):
            row = t // per_row
            c = row + (row // 2) * (circ - 4)
            base = (t % per_row) * group
            relax(pad, [(c, base + i) for i in range(group)], store)

    def outer_columns(pad, store):
        @pl.loop(1, circ // 2 - 1)
        def _(t):
            ends = (0, 1, radial - 2, radial - 1)
            relax(pad, [(2 * t + i, r) for i in range(2) for r in ends], store)

    copy_core.wait()
    copy_tiles.wait()
    inner_blocks(core0, keep)
    copy_adj.wait()
    finish_halo(0, pad0)
    outer_rows(pad0, keep)
    start_dom(1, pad1, (0, 1))
    for kind in (0, 1):
        halo(1, pad1, kind).start()
    outer_columns(pad0, keep)
    start_dom(1, pad1, (2,))
    to_smem.wait()
    inner_blocks(core1, finish)
    forward_corners(1, pad1)
    finish_halo(1, pad1)
    outer_rows(pad1, finish)
    outer_columns(pad1, finish)

    write = pltpu.make_async_copy(result, adj_out, out_sem)
    write.start()

    def gather(k):
        offset = k * per_peer % 128

        @pl.loop(0, per_peer // 16)
        def _(g):
            for i in range(16):
                p = g * 16 + i
                at = jnp.clip(ids_smem[k, 0, p + offset], 0, circ * span - 1)
                reply_f32[pl.ds(k * per_peer + p, 1), :] = final[pl.ds(at, 1), :]

    for k in reversed(range(1, dom_n)):
        gather(k)
        reply_send[part(k), :] = reply_f32[part(k), :].astype(BF16)
        back_copy(k).start()
    gather(0)
    reply_recv[part(d), :] = reply_f32[part(0), :].astype(BF16)

    drain_halo(0, pad0)
    drain_halo(1, pad1)
    for k in range(1, dom_n):
        for copy in face_copies(k):
            copy.wait_send()
    for k in range(1, dom_n):
        back_copy(k).wait()
    grad_out[0] = lax.dot_general(
        weight[...], reply_recv[...], (((0,), (0,)), ((), ())), preferred_element_type=F32
    ).astype(BF16)
    write.wait()


def solution(mesh):
    sect_n, dom_n = mesh.shape["sect"], mesh.shape["dom"]

    def shards(face_sens, face_owner, face_node, face_mask, adjoint_prev, block_rows, coupling):
        circ, radial, tile, cols = adjoint_prev.shape
        faces = face_sens.shape[1]
        per_peer = 2 * faces // dom_n
        slots = per_peer * dom_n
        nodes = circ * radial * tile
        pad = pltpu.VMEM((circ + 4, radial + 4, tile, cols), BF16)
        picks = pltpu.SMEM((circ * radial * coupling.shape[2],), jnp.int32)
        peer_sem = pltpu.SemaphoreType.DMA((dom_n,))
        vmem = pl.BlockSpec(memory_space=pltpu.VMEM)
        anywhere = pl.BlockSpec(memory_space=pl.ANY)
        codes = jnp.transpose(coupling, (2, 0, 1))
        return pl.pallas_call(
            functools.partial(kernel, sect_n, dom_n, per_peer),
            out_shape=(
                jax.ShapeDtypeStruct(adjoint_prev.shape, BF16),
                jax.ShapeDtypeStruct(face_sens.shape, BF16),
            ),
            in_specs=[anywhere] * 7,
            out_specs=(anywhere, vmem),
            scratch_shapes=[
                pltpu.VMEM(face_sens.shape, BF16),
                pltpu.VMEM(face_owner.shape, jnp.int32),
                pltpu.VMEM(face_owner.shape, jnp.int32),
                pltpu.VMEM(face_owner.shape, jnp.int32),
                pltpu.SMEM((coupling.shape[2], circ, radial), jnp.int32),
                pltpu.VMEM(adjoint_prev.shape, BF16),
                pltpu.VMEM(adjoint_prev.shape, BF16),
                pad,
                pad,
                pltpu.VMEM(block_rows.shape, BF16),
                pltpu.VMEM((nodes, cols), F32),
                pltpu.VMEM((nodes, cols), F32),
                pltpu.VMEM(adjoint_prev.shape, BF16),
                pltpu.VMEM((slots, faces), BF16),
                pltpu.VMEM((slots, cols), BF16),
                pltpu.VMEM((slots, cols), BF16),
                pltpu.VMEM((dom_n, 8, 128), jnp.int32),
                pltpu.VMEM((dom_n, 8, 128), jnp.int32),
                pltpu.VMEM((slots, cols), F32),
                pltpu.VMEM((slots, cols), BF16),
                pltpu.VMEM((slots, cols), BF16),
                pltpu.SMEM((dom_n, 8, 128), jnp.int32),
                picks,
                picks,
                pltpu.SemaphoreType.DMA((2, 12)),
                pltpu.SemaphoreType.DMA((2, 12)),
                peer_sem, peer_sem, peer_sem, peer_sem, peer_sem, peer_sem,
                pltpu.SemaphoreType.DMA((9,)),
                pltpu.SemaphoreType.DMA,
            ],
            compiler_params=pltpu.CompilerParams(
                collective_id=0, has_side_effects=True, vmem_limit_bytes=60 * 1024 * 1024
            ),
        )(face_sens, face_owner, face_node, face_mask, codes, adjoint_prev, block_rows)

    placed = (
        P("sect", "dom", None),
        P("sect", "dom"),
        P("sect", "dom"),
        P("sect", "dom"),
        P("sect", "dom", None, None),
        P("sect", "dom", None, None),
        P("sect", "dom", None),
    )
    return jax.shard_map(
        shards,
        mesh=mesh,
        in_specs=placed,
        out_specs=(P("sect", "dom", None, None), P("sect", "dom", None)),
        check_vma=False,
    )
```
